256 devices in a mesh: dp: 32 (over z, y), tensor: 8 (over x, core).
Axes of the slice: x: 4, y: 4, z: 8, core: 2. Of those that a mesh axis runs over, the one named last changes fastest.
Arguments:
- queries: bfloat16 [16384, 8192], P('dp', 'tensor'), may hold values from -200 to 200
- keys: bfloat16 [16384, 1024], P('dp', 'tensor'), may hold values from -6 to 6
- values: bfloat16 [16384, 1024], P('dp', 'tensor'), may hold values from -6 to 6
- outputs: bfloat16 [16384, 8192], P('dp', 'tensor'), may hold values from -2 to 2
- out_grad: bfloat16 [16384, 8192], P('dp', 'tensor'), may hold values from -24 to 24
- prefix_key: bfloat16 [8, 256, 128], P('tensor'), may hold values from -6 to 6
- prefix_value: bfloat16 [8, 256, 128], P('tensor'), may hold values from -6 to 6
- w_query: bfloat16 [8192, 8192], P('dp', 'tensor'), may hold values from -0.0625 to 0.0625
- w_key: bfloat16 [8192, 1024], P('dp', 'tensor'), may hold values from -0.1875 to 0.1875
- w_value: bfloat16 [8192, 1024], P('dp', 'tensor'), may hold values from -0.1875 to 0.1875
Outputs:
- input_grad: bfloat16 [16384, 8192], P('dp', 'tensor')
- prefix_key_grad: float32 [8, 256, 128], P('tensor')
- prefix_value_grad: float32 [8, 256, 128], P('tensor')
The draws below stay inside these ranges and needn't reach their ends.
All inputs are finite; a program needn't handle non-finite values.
Results may differ from the reference program's by a relative error of at most 0.02.
Values may be sent and summed in bfloat16 or wider, within the bound.
No kernel may reach another device: no remote copies, remote signals or barrier semaphores. Data moves between devices by JAX's collectives and lax.ppermute only.
A program may use at most 128 MiB of HBM per device.

```python
import math
import jax
import jax.numpy as jnp
from jax import lax

D = 8192
HQ = 64
KVH = 8
HD = 128
P_SIZE = 256
LEN = 256
REQUESTS = 64
TOKENS = 16384
N_TENSOR = 8


def shared_keys(key):
    return jnp.clip(jax.random.normal(key, (KVH, P_SIZE, HD), jnp.float32), -6.0, 6.0)


def draw_prefix_key(key, part):
    base = shared_keys(key)
    return base.astype(jnp.bfloat16)


def draw_queries(key, part):
    key = jax.random.fold_in(key, 9)
    noise = jnp.clip(jax.random.normal(key, (TOKENS, HQ, HD), jnp.float32), -6.0, 6.0)
    return noise.reshape(TOKENS, HQ * HD).astype(jnp.bfloat16)


def shard_levels(key, dims, split, least, top_value):
    loudness = 1.0
    for dim, blocks in split:
        draws = jax.random.uniform(jax.random.fold_in(jax.random.fold_in(key, 6), dim), (blocks,), jnp.float32, least / len(split), top_value / len(split))
        loudness = loudness * jnp.repeat(jnp.exp(draws), dims[dim] // blocks).reshape((-1,) + (1,) * (len(dims) - 1 - dim))
    return loudness


def centred(rng, extent, deviation, limit, cuts=(), held_as=jnp.bfloat16):
    drawn = jax.random.normal(rng, extent, jnp.float32) * deviation
    if len(cuts) > 0:
        drawn = shard_levels(rng, extent, cuts, -0.22, 0.18) * drawn
    return jnp.clip(drawn, min=-limit, max=limit).astype(held_as)


def setup_inputs(seed: int = 0) -> dict:
    arg_keys = jax.random.split(jax.random.key(seed), 11)
    queries = draw_queries(jax.random.fold_in(arg_keys[10], 71), 0)
    keys = centred(arg_keys[1], (TOKENS, KVH * HD), 1.0, 6.0, ((0, 32), (1, 8)))
    values = centred(arg_keys[2], (TOKENS, KVH * HD), 1.0, 6.0, ((0, 32), (1, 8)))
    outputs = centred(arg_keys[3], (TOKENS, HQ * HD), 0.3, 2.0, ((0, 32), (1, 8)))
    out_grad = centred(arg_keys[4], (TOKENS, HQ * HD), 4.0, 24.0, ((0, 32), (1, 8)))
    prefix_key = draw_prefix_key(jax.random.fold_in(arg_keys[10], 71), 0)
    prefix_value = centred(arg_keys[6], (KVH, P_SIZE, HD), 1.0, 6.0, ((0, 8),))
    w_query = centred(arg_keys[7], (D, HQ * HD), (HQ * HD) ** -0.5, 0.0625, ((0, 32), (1, 8)))
    w_key = centred(arg_keys[8], (D, KVH * HD), (KVH * HD) ** -0.5, 0.1875, ((0, 32), (1, 8)))
    w_value = centred(arg_keys[9], (D, KVH * HD), (KVH * HD) ** -0.5, 0.1875, ((0, 32), (1, 8)))
    return dict(queries=queries, keys=keys, values=values, outputs=outputs, out_grad=out_grad, prefix_key=prefix_key, prefix_value=prefix_value, w_query=w_query, w_key=w_key, w_value=w_value)


def attend_request(query_blk, key_blk, value_blk, output_blk, grad_blk, prefix_key, prefix_value):
    scale = 1.0 / math.sqrt(HD)
    keyset = jnp.concatenate([jnp.transpose(prefix_key, (1, 0, 2)), key_blk], axis=0).astype(jnp.float32)
    valueset = jnp.concatenate([jnp.transpose(prefix_value, (1, 0, 2)), value_blk], axis=0).astype(jnp.float32)
    query_full = query_blk.astype(jnp.float32)
    grad_full = grad_blk.astype(jnp.float32)
    output_full = output_blk.astype(jnp.float32)
    scores = jnp.einsum('tkgd,skd->kgts', query_full, keyset) * scale
    column = jnp.arange(P_SIZE + LEN)[None, :]
    row_pos = jnp.arange(LEN)[:, None]
    allowed = (column < P_SIZE) | (column - P_SIZE <= row_pos)
    scores = jnp.where(allowed, scores, -jnp.inf)
    highest = lax.optimization_barrier(jnp.max(scores, axis=-1, keepdims=True))
    expo = jnp.exp(scores - highest)
    probs = expo / lax.optimization_barrier(jnp.sum(expo, axis=-1, keepdims=True))
    probs_b = lax.optimization_barrier(probs.astype(jnp.bfloat16)).astype(jnp.float32)
    delta = jnp.transpose(lax.optimization_barrier(jnp.sum(grad_full * output_full, axis=-1)), (1, 2, 0))
    dprob = jnp.einsum('tkgd,skd->kgts', grad_full, valueset)
    dscore = probs * (dprob - delta[..., None])
    dscore_b = lax.optimization_barrier(dscore.astype(jnp.bfloat16)).astype(jnp.float32)
    query_grad = (jnp.einsum('kgts,skd->tkgd', dscore_b, keyset) * scale).astype(jnp.bfloat16)
    keyset_grad = jnp.einsum('kgts,tkgd->skd', dscore_b, query_full) * scale
    valueset_grad = jnp.einsum('kgts,tkgd->skd', probs_b, grad_full)
    return (query_grad, keyset_grad[P_SIZE:].astype(jnp.bfloat16), valueset_grad[P_SIZE:].astype(jnp.bfloat16), keyset_grad[:P_SIZE], valueset_grad[:P_SIZE])

def reference(queries, keys, values, outputs, out_grad, prefix_key, prefix_value, w_query, w_key, w_value):
    group = HQ // KVH
    shape_five = (REQUESTS, LEN, KVH, group, HD)
    shape_four = (REQUESTS, LEN, KVH, HD)
    stacked = (queries.reshape(shape_five), keys.reshape(shape_four), values.reshape(shape_four), outputs.reshape(shape_five), out_grad.reshape(shape_five))

    def step(carry, items):
        results = attend_request(items[0], items[1], items[2], items[3], items[4], prefix_key, prefix_value)
        return ((carry[0] + results[3], carry[1] + results[4]), (results[0], results[1], results[2]))
    start = (jnp.zeros((P_SIZE, KVH, HD), jnp.float32), jnp.zeros((P_SIZE, KVH, HD), jnp.float32))
    sums, grads = lax.scan(step, start, stacked)
    query_grad = grads[0].reshape(TOKENS, HQ * HD)
    key_grad = grads[1].reshape(TOKENS, KVH * HD)
    value_grad = grads[2].reshape(TOKENS, KVH * HD)
    query_cols = HQ * HD // N_TENSOR
    key_cols = KVH * HD // N_TENSOR
    total = jnp.zeros((TOKENS, D), jnp.float32)
    for index in range(N_TENSOR):
        qlo = index * query_cols
        klo = index * key_cols
        term = jnp.dot(query_grad[:, qlo:qlo + query_cols], w_query[:, qlo:qlo + query_cols].T, preferred_element_type=jnp.float32)
        term = term + jnp.dot(key_grad[:, klo:klo + key_cols], w_key[:, klo:klo + key_cols].T, preferred_element_type=jnp.float32)
        term = term + jnp.dot(value_grad[:, klo:klo + key_cols], w_value[:, klo:klo + key_cols].T, preferred_element_type=jnp.float32)
        total = total + lax.optimization_barrier(term.astype(jnp.bfloat16)).astype(jnp.float32)
    input_grad = total.astype(jnp.bfloat16)
    return (input_grad, jnp.transpose(sums[0], (1, 0, 2)), jnp.transpose(sums[1], (1, 0, 2)))
```

```python
import math

import jax
import jax.numpy as jnp
from jax import lax
from jax.experimental import pallas as pl
from jax.experimental.pallas import tpu as pltpu
from jax.sharding import Mesh
from jax.sharding import PartitionSpec as P

LEN = 256
HEADS = 8
HD = 128
NZ, NY, NX, NC = 8, 4, 4, 2
MIB = 1024 * 1024
VMEM_SMALL = 16 * MIB
VMEM_PRODUCT = 24 * MIB
SMALL = pl.CostEstimate(flops=1024, bytes_accessed=1024, transcendentals=0)
NT_DIMS = (((1,), (1,)), ((), ()))


def attend_kernel(
    q_ref, k_ref, v_ref, o_ref, g_ref, pk_ref, pv_ref, grad_ref, sum_ref, pre_ref, keyset, valueset, dk_acc, dv_acc
):
    req = pl.program_id(0)
    prefix = pk_ref.shape[1]
    rows = pl.ds(pl.multiple_of(req * LEN, LEN), LEN)
    scale = 1.0 / math.sqrt(HD)
    unit = scale * math.log2(math.e)
    keyset[:prefix] = pk_ref[0]
    keyset[prefix:] = k_ref[...]
    valueset[:prefix] = pv_ref[0]
    valueset[prefix:] = v_ref[...]
    lane = lax.broadcasted_iota(jnp.int32, (LEN, HD), 1)
    spread = jnp.zeros((LEN, HD), jnp.float32)
    for h in range(HEADS):
        cols = pl.ds(h * HD, HD)
        delta = jnp.sum(
            g_ref[:, cols].astype(jnp.float32) * o_ref[:, cols].astype(jnp.float32),
            axis=1,
            keepdims=True,
        )
        spread = jnp.where(lane == h, delta, spread)
    deltas = spread.T
    key_pos = lax.broadcasted_iota(jnp.int32, (LEN, LEN), 0)
    tok_pos = lax.broadcasted_iota(jnp.int32, (LEN, LEN), 1)
    seen = key_pos <= tok_pos
    keys = keyset[...]
    vals = valueset[...]
    for h in range(HEADS):
        cols = pl.ds(h * HD, HD)
        q = q_ref[:, cols]
        g = g_ref[:, cols]
        s = lax.dot_general(keys, q, NT_DIMS, preferred_element_type=jnp.float32)
        s_a = s[:prefix]
        s_b = jnp.where(seen, s[prefix:], -jnp.inf)
        top = jnp.maximum(
            jnp.max(s_a, axis=0, keepdims=True), jnp.max(s_b, axis=0, keepdims=True)
        )
        e_a = jnp.exp2((s_a - top) * unit)
        e_b = jnp.exp2((s_b - top) * unit)
        total = jnp.sum(e_a, axis=0, keepdims=True) + jnp.sum(e_b, axis=0, keepdims=True)
        inv = 1.0 / total
        probs = jnp.concatenate([e_a * inv, e_b * inv], axis=0)
        dprob = lax.dot_general(vals, g, NT_DIMS, preferred_element_type=jnp.float32)
        dscore = (probs * (dprob - deltas[h : h + 1, :])).astype(jnp.bfloat16)
        probs_b = probs.astype(jnp.bfloat16)
        dq = lax.dot_general(
            dscore, keys, (((0,), (0,)), ((), ())), preferred_element_type=jnp.float32
        )
        grad_ref[rows, cols] = (dq * scale).astype(jnp.bfloat16)
        dk = jnp.dot(dscore, q, preferred_element_type=jnp.float32)
        dv = jnp.dot(probs_b, g, preferred_element_type=jnp.float32)
        if h == 0:
            dk_acc[...] = dk
            dv_acc[...] = dv
        else:
            dk_acc[...] += dk
            dv_acc[...] += dv
    width = HEADS * HD
    grad_ref[rows, pl.ds(width, HD)] = (dk_acc[prefix:] * scale).astype(jnp.bfloat16)
    grad_ref[rows, pl.ds(width + HD, HD)] = dv_acc[prefix:].astype(jnp.bfloat16)

    @pl.when(req == 0)
    def _():
        pre_ref[:prefix] = dk_acc[:prefix] * scale
        pre_ref[prefix:] = dv_acc[:prefix]

    @pl.when(req == pl.num_programs(0) - 1)
    def _():
        pre_ref[:prefix] += dk_acc[:prefix] * scale
        pre_ref[prefix:] += dv_acc[:prefix]
        sum_ref[...] = pre_ref[...].astype(jnp.bfloat16)


def attend(q, k, v, o, g, pk, pv):
    prefix = pk.shape[1]
    tokens, width = q.shape
    wide = pl.BlockSpec((LEN, width), lambda i: (i, 0))
    slim = pl.BlockSpec((LEN, HD), lambda i: (i, 0))
    pre = pl.BlockSpec((1, prefix, HD), lambda i: (0, 0, 0))
    return pl.pallas_call(
        attend_kernel,
        grid=(tokens // LEN,),
        in_specs=[wide, slim, slim, wide, wide, pre, pre],
        out_specs=[
            pl.BlockSpec((tokens, width + 2 * HD), lambda i: (0, 0)),
            pl.BlockSpec((2 * prefix, HD), lambda i: (0, 0)),
        ],
        out_shape=[
            jax.ShapeDtypeStruct((tokens, width + 2 * HD), jnp.bfloat16),
            jax.ShapeDtypeStruct((2 * prefix, HD), jnp.bfloat16),
        ],
        scratch_shapes=[pltpu.VMEM((2 * prefix, HD), jnp.float32)]
        + [pltpu.VMEM((prefix + LEN, HD), jnp.bfloat16)] * 2
        + [pltpu.VMEM((prefix + LEN, HD), jnp.float32)] * 2,
        compiler_params=pltpu.CompilerParams(vmem_limit_bytes=56 * MIB),
        cost_estimate=SMALL,
    )(q, k, v, o, g, pk, pv)


def product_kernel(offsets, counts, sizes, phases, base, extra, *refs):
    z, x, c = lax.axis_index("z"), lax.axis_index("x"), lax.axis_index("c")
    parts = refs[: sum(counts)]
    rest = refs[sum(counts) :]
    grads = rest[: len(sizes)]
    rest = rest[len(sizes) + extra :]
    outs = rest[:8]
    stamp, wbuf, gbuf, wsem, gsem, osem = rest[8:14]
    obufs = rest[14:]
    stamp[...] = jnp.zeros_like(stamp)
    width = wbuf.shape[0] // len(counts)

    def w_wait(tile):
        where = wbuf.at[pl.ds(pl.multiple_of(tile * width, width), width)]
        pltpu.make_async_copy(where, where, wsem.at[tile]).wait()

    w_copies = []
    at = 0
    for tile, count in enumerate(counts):
        row = tile * width
        w_copies.append([])
        for _ in range(count):
            src = parts[at]
            dst = wbuf.at[pl.ds(row, src.shape[0])]
            w_copies[-1].append(pltpu.make_async_copy(src, dst, wsem.at[tile]))
            row += src.shape[0]
            at += 1
    g_copies = []
    row = 0
    for blk, size in enumerate(sizes):
        src = grads[blk].at[:, pl.ds(0, gbuf.shape[1])]
        g_copies.append(pltpu.make_async_copy(src, gbuf.at[pl.ds(row, size)], gsem.at[blk]))
        row += size

    def blocks_of(phase):
        at = 0
        for blk, size in enumerate(sizes):
            if at < phase[3] + phase[4] and at + size > phase[3]:
                yield blk
            at += size

    def tiles_of(phase):
        return range(phase[0], phase[0] + phase[1] * phase[2])

    started = set()
    for phase in phases:
        for blk in blocks_of(phase):
            if blk not in started:
                g_copies[blk].start()
                started.add(blk)
        for tile in tiles_of(phase):
            if -1 - tile not in started:
                for copy in w_copies[tile]:
                    copy.start()
                started.add(-1 - tile)

    ended = set()
    drains = []
    for which, phase in enumerate(phases):
        tile_0, groups, per, first, rows = phase
        for blk in blocks_of(phase):
            if blk not in ended:
                g_copies[blk].wait()
                ended.add(blk)
        fresh = -1 - tile_0 not in ended
        for tile in tiles_of(phase):
            ended.add(-1 - tile)
        obuf = obufs[which]
        where = pl.ds(base + first, rows)

        def copy_out(slot, k, value, obuf=obuf, where=where, which=which):
            return pltpu.make_async_copy(
                obuf.at[slot, :, pl.ds(k * width, width)], outs[value].at[where], osem.at[which, slot, k]
            )

        def one(i):
            slot = lax.rem(i, 2)

            @pl.when(i >= 2)
            def _():
                for k in range(per):
                    copy_out(slot, k, 0).wait()

            if fresh:
                for k in range(per):
                    w_wait(tile_0 + i * per + k)
            start = pl.multiple_of((tile_0 + i * per) * width, width)
            obuf[slot] = lax.dot_general(
                gbuf[pl.ds(first, rows), :],
                wbuf[pl.ds(start, per * width), :],
                NT_DIMS,
                preferred_element_type=jnp.float32,
            ).astype(jnp.bfloat16)
            for k in range(per):
                tile = tile_0 + i * per + k
                off = jnp.int32(offsets[0])
                for t in range(1, len(offsets)):
                    off = jnp.where(tile == t, jnp.int32(offsets[t]), off)
                row = lax.rem(z + off, NZ)
                rel = lax.rem(lax.div(row, 2) - x + NX, NX)
                place = rel + jnp.where(lax.rem(row, 2) == c, 4, 0)
                for value in range(8):
                    @pl.when(place == value)
                    def _():
                        copy_out(slot, k, value).start()

        pl.loop(0, groups)(one)
        drains += [(copy_out, slot, k) for slot in range(min(2, groups)) for k in range(per)]
    for copy_out, slot, k in drains:
        copy_out(slot, k, 0).wait()


def product(offsets, tiles, grads, phases, base, total, prev=None, deps=()):
    counts = [len(tile) for tile in tiles]
    flat = [part for tile in tiles for part in tile]
    rows = sum(part.shape[0] for part in tiles[0])
    depth = flat[0].shape[1]
    sizes = [g.shape[0] for g in grads]
    anywhere = pl.BlockSpec(memory_space=pl.ANY)
    hbm = pl.BlockSpec(memory_space=pltpu.HBM)
    args = [*flat, *grads]
    given = len(args)
    aliases = {}
    if prev is not None:
        aliases = {len(args) + i: i for i in range(8)}
        args += list(prev)
    args += list(deps)
    extra = len(args) - len(flat) - len(grads)

    def body(*refs):
        product_kernel(offsets, counts, sizes, phases, base, extra, *refs)

    results = pl.pallas_call(
        body,
        in_specs=[hbm] * given + [anywhere] * (len(args) - given),
        out_specs=[anywhere] * 8 + [pl.BlockSpec(memory_space=pltpu.VMEM)],
        out_shape=[jax.ShapeDtypeStruct((total, rows), jnp.bfloat16)] * 8
        + [jax.ShapeDtypeStruct((8, 128), jnp.float32)],
        input_output_aliases=aliases,
        scratch_shapes=[
            pltpu.VMEM((len(tiles) * rows, depth), jnp.bfloat16),
            pltpu.VMEM((sum(sizes), depth), jnp.bfloat16),
            pltpu.SemaphoreType.DMA((len(tiles),)),
            pltpu.SemaphoreType.DMA((len(grads),)),
            pltpu.SemaphoreType.DMA((len(phases), 2, max(phase[2] for phase in phases))),
        ]
        + [pltpu.VMEM((2, phase[4], phase[2] * rows), jnp.bfloat16) for phase in phases],
        compiler_params=pltpu.CompilerParams(vmem_limit_bytes=VMEM_PRODUCT),
        cost_estimate=SMALL,
    )(*args)
    return results[:-1], results[-1]


def pack_kernel(a_ref, b_ref, c_ref, out_ref):
    at = 0
    for ref in (a_ref, b_ref, c_ref):
        out_ref[:, pl.ds(at, ref.shape[1])] = ref[...]
        at += ref.shape[1]


def pack(*parts):
    width = sum(part.shape[1] for part in parts)
    return pl.pallas_call(
        pack_kernel,
        out_shape=jax.ShapeDtypeStruct((parts[0].shape[0], width), parts[0].dtype),
        compiler_params=pltpu.CompilerParams(vmem_limit_bytes=56 * MIB),
        cost_estimate=SMALL,
    )(*parts)


def lay_kernel(*refs):
    y = lax.axis_index("y")
    out_ref = refs[NY]
    for i, ref in enumerate(refs[:NY]):
        width = ref.shape[1]
        start = pl.multiple_of(lax.rem(y + i, NY) * width, width)
        out_ref[:, pl.ds(start, width)] = ref[...]


def lay(pieces):
    rows, width = pieces[0].shape
    whole = pl.BlockSpec((rows, width), lambda: (0, 0))
    return pl.pallas_call(
        lay_kernel,
        in_specs=[whole] * NY,
        out_shape=jax.ShapeDtypeStruct((rows, NY * width), pieces[0].dtype),
        compiler_params=pltpu.CompilerParams(vmem_limit_bytes=VMEM_SMALL),
        cost_estimate=SMALL,
    )(*pieces)


def cut_kernel(*refs):
    for src, dst in zip(refs[:4], refs[4:], strict=True):
        dst[...] = src[...]


def cut(*pairs):
    arrays = [array for pair in pairs for array in pair]

    def spec(array, at):
        return pl.BlockSpec((array.shape[0] // 2, array.shape[1]), lambda i: (at, 0))

    return pl.pallas_call(
        cut_kernel,
        grid=(1,),
        in_specs=[spec(array, i % 2) for i, array in enumerate(arrays)],
        out_specs=[spec(array, 0) for array in arrays],
        out_shape=[
            jax.ShapeDtypeStruct((a.shape[0] // 2, a.shape[1]), a.dtype) for a in arrays
        ],
        compiler_params=pltpu.CompilerParams(vmem_limit_bytes=VMEM_SMALL),
        cost_estimate=SMALL,
    )(*arrays)


def add_refs(*refs):
    total = refs[0].astype(jnp.float32)
    for ref in refs[1:]:
        total = total + ref.astype(jnp.float32)
    return total.astype(jnp.bfloat16)


def by_rows(kernel, rows, first, tokens, args, widths, deps=()):
    def spec(array):
        skip = first // rows if array.shape[0] > tokens else 0
        return pl.BlockSpec((rows, array.shape[1]), lambda i: (i + skip, 0))

    shapes = [jax.ShapeDtypeStruct((tokens, width), jnp.bfloat16) for width in widths]
    return pl.pallas_call(
        kernel,
        grid=(tokens // rows,),
        in_specs=[spec(arg) for arg in args] + [pl.BlockSpec(memory_space=pl.ANY)] * len(deps),
        out_specs=[spec(shape) for shape in shapes],
        out_shape=shapes,
        compiler_params=pltpu.CompilerParams(vmem_limit_bytes=VMEM_SMALL),
        cost_estimate=SMALL,
    )(*args, *deps)


def far_kernel(keep, got, *refs):
    a_ref, b_ref = refs[-2:]
    half = a_ref.shape[1]
    a_ref[...] = add_refs(keep[:, :half], got[:, :half])
    b_ref[...] = add_refs(keep[:, half:], got[:, half:])


def near_kernel(keep_up, got_up, far_up, keep_down, got_down, far_down, *refs):
    up, down = refs[-2:]
    half = far_up.shape[1]
    up[:, :half] = add_refs(keep_up[:, :half], got_up[:, :half], far_up[...])
    up[:, half:] = add_refs(keep_up[:, half:], got_up[:, half:])
    down[:, :half] = add_refs(keep_down[:, :half], got_down[:, :half])
    down[:, half:] = add_refs(keep_down[:, half:], got_down[:, half:], far_down[...])


def total_kernel(keep, got, up, down, out):
    out[...] = add_refs(keep[...], got[...], up[...], down[...])


def total(row, row_got, rows, keep, got, up, down):
    def spec(first):
        at = first // rows
        return pl.BlockSpec((rows, keep.shape[1]), lambda i: (at, 0))

    return pl.pallas_call(
        total_kernel,
        grid=(1,),
        in_specs=[spec(row), spec(row), spec(row_got), spec(row_got)],
        out_specs=spec(0),
        out_shape=jax.ShapeDtypeStruct((rows, keep.shape[1]), jnp.bfloat16),
        compiler_params=pltpu.CompilerParams(vmem_limit_bytes=VMEM_SMALL),
        cost_estimate=SMALL,
    )(keep, got, up, down)


def prefix_kernel(own, other, *refs):
    refs[-1][...] = (own[...].astype(jnp.float32) + other[...].astype(jnp.float32)).astype(
        refs[-1].dtype
    )


def prefix_add(own, other, dtype, *deps):
    whole = pl.BlockSpec(memory_space=pltpu.VMEM)
    return pl.pallas_call(
        prefix_kernel,
        in_specs=[whole] * 2 + [pl.BlockSpec(memory_space=pl.ANY)] * len(deps),
        out_specs=whole,
        out_shape=jax.ShapeDtypeStruct(own.shape, dtype),
        compiler_params=pltpu.CompilerParams(vmem_limit_bytes=VMEM_SMALL),
        cost_estimate=SMALL,
    )(own, other, *deps)


def shift(value, axis, size, by):
    return lax.ppermute(value, axis, [(i, (i + by) % size) for i in range(size)])


def swap(value, axis, size, mask):
    return lax.ppermute(value, axis, [(i, i ^ mask) for i in range(size)])


def shards(
    queries, keys, values, outputs, out_grad, prefix_key, prefix_value, w_query, w_key, w_value
):
    tokens = queries.shape[0]
    every = NY * tokens
    weight = pack(w_query, w_key, w_value)

    tiles = {0: (weight,)}
    with jax.named_scope("weights"):
        up = down = weight
        for step in range(1, 4):
            up = shift(up, "z", NZ, 1)
            down = shift(down, "z", NZ, -1)
            tiles[NZ - step], tiles[step] = (up,), (down,)

    grad, prefix_sum = attend(
        queries, keys, values, outputs, out_grad, prefix_key, prefix_value
    )
    with jax.named_scope("grads"):
        g_up = shift(grad, "y", NY, 1)
        g_down = shift(grad, "y", NY, -1)
    up_half, down_half, up_tile, down_tile = cut((g_up, g_down), (up, down))
    with jax.named_scope("grads_far"):
        far_a = shift(up_half, "y", NY, 1)
        far_b = shift(down_half, "y", NY, -1)
    with jax.named_scope("weights_far"):
        tiles[4] = (shift(up_tile, "z", NZ, 1), shift(down_tile, "z", NZ, -1))

    near = [g_up, grad, g_down]
    rest = every - tokens
    offsets = [0, 1, 7, 2, 6, 3, 5, 4]
    part, stamp = product(
        offsets[:7],
        [tiles[off] for off in offsets[:7]],
        near,
        [(0, 3, 2, 0, rest), (6, 1, 1, 0, rest)],
        tokens,
        every,
    )
    part, _ = product(
        offsets,
        [tiles[off] for off in offsets],
        [far_a, far_b, *near],
        [(0, 2, 4, 0, tokens), (7, 1, 1, tokens, rest)],
        0,
        every,
        part,
        deps=(stamp,),
    )

    send, keep = part[:4], part[4:]
    with jax.named_scope("sum_c"):
        got = {rel: swap(send[rel], "c", NC, 1) for rel in (2, 1, 3, 0)}
    width = keep[0].shape[1]
    far_sum = by_rows(far_kernel, 2 * LEN, 0, every, [keep[2], got[2]], [width // 2] * 2)
    with jax.named_scope("sum_x1"):
        far_up = shift(far_sum[0], "x", NX, 1)
        far_down = shift(far_sum[1], "x", NX, -1)
    args = [keep[1], got[1], far_up, keep[3], got[3], far_down]
    prefix = prefix_sum
    with jax.named_scope("prefix"):
        prefix = prefix_add(prefix, swap(prefix, "z", NZ, 1), jnp.bfloat16)
        prefix = prefix_add(prefix, swap(prefix, "z", NZ, 2), jnp.bfloat16)
    dep = (prefix,)
    sums = []
    for first in (0, every // 2):
        ways = by_rows(near_kernel, 2 * LEN, first, every // 2, args, [width] * 2, dep)
        dep = (ways[0],)
        with jax.named_scope("sum_x2"):
            got_up = shift(ways[0], "x", NX, 1)
            got_down = shift(ways[1], "x", NX, -1)
        for part_first in (0, tokens):
            sums.append((first + part_first, part_first, got_up, got_down))
    blocks = []
    for row, row_got, got_up, got_down in sums:
        blocks.append(total(row, row_got, tokens, keep[0], got[0], got_up, got_down))
    from_far, from_up, own, from_down = blocks

    with jax.named_scope("prefix"):
        prefix = prefix_add(prefix, swap(prefix, "z", NZ, 4), jnp.bfloat16, *dep)
        prefix = prefix_add(prefix, swap(prefix, "y", NY, 1), jnp.bfloat16)
        prefix_total = prefix_add(prefix, swap(prefix, "y", NY, 2), jnp.float32)

    with jax.named_scope("back"):
        back_far = shift(from_far, "y", NY, 2)
        back_up = shift(from_up, "y", NY, -1)
        back_down = shift(from_down, "y", NY, 1)
    input_grad = lay([own, back_up, back_far, back_down])
    prefix_len = prefix_key.shape[1]
    return (input_grad, prefix_total[None, :prefix_len], prefix_total[None, prefix_len:])


def solution(mesh):
    fine = Mesh(mesh.devices.reshape(NZ, NY, NX, NC), ("z", "y", "x", "c"))
    full = P(("z", "y"), ("x", "c"))
    head = P(("x", "c"), None, None)
    return jax.shard_map(
        shards,
        mesh=fine,
        in_specs=(full, full, full, full, full, head, head, full, full, full),
        out_specs=(full, head, head),
        check_vma=False,
    )
```
